32 devices in a mesh: ctx: 8 (over z, x), kvh: 4 (over y, core).
Axes of the slice: x: 2, y: 2, z: 4, core: 2. Of those that a mesh axis runs over, the one named last changes fastest.
Arguments:
- query_act: bfloat16 [2048, 8192], P(('ctx', 'kvh')), may hold values from -6 to 6
- key_act: bfloat16 [2048, 1024], P(('ctx', 'kvh')), may hold values from -6 to 6
- value_act: bfloat16 [2048, 1024], P(('ctx', 'kvh')), may hold values from -6 to 6
- grad_out: bfloat16 [2048, 8192], P(('ctx', 'kvh')), may hold values from -6 to 6
Outputs:
- attn_out: bfloat16 [2048, 8192], P(('ctx', 'kvh'))
- grad_query: bfloat16 [2048, 8192], P(('ctx', 'kvh'))
- grad_key: bfloat16 [2048, 1024], P(('ctx', 'kvh'))
- grad_value: bfloat16 [2048, 1024], P(('ctx', 'kvh'))
The draws below stay inside these ranges and needn't reach their ends.
All inputs are finite; a program needn't handle non-finite values.
Results may differ from the reference program's by a relative error of at most 0.014.
Values may be sent and summed in bfloat16 or wider, within the bound.
No kernel may reach another device: no remote copies, remote signals or barrier semaphores. Data moves between devices by JAX's collectives and lax.ppermute only.
A program may use at most 128 MiB of HBM per device.

```python
import jax
import jax.numpy as jnp
from jax import lax

KVH = 8
QPK = 8
HD = 128
BLK = 256
SEQ = 2048
LEVELS = 3
N_CTX = 8


def draw_query_act(key, part):
    rows_total = BLK * N_CTX
    base = jax.random.normal(jax.random.fold_in(key, 11), (rows_total, KVH * QPK * HD), jnp.float32)
    return jnp.clip(base, -6.0, 6.0).astype(jnp.bfloat16)


def draw_key_act(key, part):
    rows_total = BLK * N_CTX
    base = jax.random.normal(jax.random.fold_in(key, 21), (rows_total, KVH * HD), jnp.float32)
    return jnp.clip(base, -6.0, 6.0).astype(jnp.bfloat16)


def steps_of(stream_key, shape, split, low, high):
    def one(dim, parts):
        steps = jax.random.uniform(jax.random.fold_in(jax.random.fold_in(stream_key, 6), dim), (parts,), jnp.float32, low / len(split), high / len(split))
        return jnp.repeat(jnp.exp(steps), shape[dim] // parts).reshape((-1,) + (1,) * (len(shape) - dim - 1))

    factor_of = one(*split[0])
    for cut in split[1:]:
        factor_of = factor_of * one(*cut)
    return factor_of


def scatter_about(own_key, dims, scale, most, cuts=(), dtype=jnp.bfloat16):
    factor_of = steps_of(own_key, dims, cuts, -0.22, 0.18) if cuts else 1.0
    drawn = jax.random.normal(own_key, dims, jnp.float32) * scale * factor_of
    return jnp.minimum(jnp.maximum(drawn, -most), most).astype(dtype)


def setup_inputs(seed: int = 0) -> dict:
    keys = jax.random.split(jax.random.key(seed), 5)
    query_act = draw_query_act(jax.random.fold_in(keys[4], 71), 0)
    key_act = draw_key_act(jax.random.fold_in(keys[4], 71), 0)
    value_act = scatter_about(keys[2], (SEQ, KVH * HD), 1.0, 6.0, ((0, 32),))
    grad_out = scatter_about(keys[3], (SEQ, KVH * QPK * HD), 1.0, 6.0, ((0, 32),))
    return dict(query_act=query_act, key_act=key_act, value_act=value_act, grad_out=grad_out)


masked_score = -1e30


def reference(query_act, key_act, value_act, grad_out):
    scale = HD ** -0.5
    queries = query_act.reshape(N_CTX, BLK, KVH, QPK, HD)
    key_rows = key_act.reshape(N_CTX, BLK, KVH, HD)
    value_rows = value_act.reshape(N_CTX, BLK, KVH, HD)
    grad_rows = grad_out.reshape(N_CTX, BLK, KVH, QPK, HD)
    position = jnp.arange(BLK)
    causal = (position[None, :] <= position[:, None])[None, None]

    def one_block(carry, block):
        key_grad_all, value_grad_all = carry
        q_block = queries[block].astype(jnp.float32)
        g_block = grad_rows[block].astype(jnp.float32)
        listing = [(block, causal)]
        for level in range(LEVELS):
            distance = 1 << level
            source = jnp.maximum(block - distance, 0).astype(jnp.int32)
            valid = jnp.broadcast_to(block >= distance, (1, 1, 1, 1))
            listing.append((source, valid))
        scores_all = []
        maxima = []
        sums = []
        outs_all = []
        for source, mask in listing:
            key_f = key_rows[source].astype(jnp.float32)
            val_f = value_rows[source].astype(jnp.float32)
            scores = jnp.einsum('tgrd,ugd->grtu', q_block, key_f) * scale
            scores = jnp.where(mask, scores, masked_score)
            level_max = jnp.max(scores, axis=3)
            expo = jnp.where(mask, jnp.exp(scores - level_max[..., None]), 0.0)
            level_sum = jnp.sum(expo, axis=3)
            weights = expo.astype(jnp.bfloat16).astype(jnp.float32)
            level_out = jnp.einsum('grtu,ugd->tgrd', weights, val_f)
            scores_all.append(scores)
            maxima.append(level_max)
            sums.append(level_sum)
            outs_all.append(level_out)
        top = maxima[0]
        for level_max in maxima[1:]:
            top = jnp.maximum(top, level_max)
        total = jnp.zeros_like(top)
        acc = jnp.zeros_like(outs_all[0])
        for level_max, level_sum, level_out in zip(maxima, sums, outs_all):
            factor = jnp.exp(level_max - top)
            total = total + factor * level_sum
            acc = acc + jnp.transpose(factor, (2, 0, 1))[..., None] * level_out
        logsum = top + jnp.log(total)
        out_block = (acc / jnp.transpose(total, (2, 0, 1))[..., None]).astype(jnp.bfloat16)
        delta = jnp.transpose(jnp.sum(g_block * out_block.astype(jnp.float32), axis=3), (1, 2, 0))
        grad_q = jnp.zeros_like(q_block)
        for (source, mask), scores in zip(listing, scores_all):
            key_f = key_rows[source].astype(jnp.float32)
            val_f = value_rows[source].astype(jnp.float32)
            probs = jnp.where(mask, jnp.exp(scores - logsum[..., None]), 0.0)
            probs_low = probs.astype(jnp.bfloat16).astype(jnp.float32)
            grad_val = jnp.einsum('grtu,tgrd->ugd', probs_low, g_block)
            grad_prob = jnp.einsum('tgrd,ugd->grtu', g_block, val_f)
            grad_scores = (probs * (grad_prob - delta[..., None])).astype(jnp.bfloat16).astype(jnp.float32)
            grad_q = grad_q + scale * jnp.einsum('grtu,ugd->tgrd', grad_scores, key_f)
            grad_k = scale * jnp.einsum('grtu,tgrd->ugd', grad_scores, q_block)
            key_grad_all = key_grad_all.at[source].add(grad_k)
            value_grad_all = value_grad_all.at[source].add(grad_val)
        return (key_grad_all, value_grad_all), (out_block, grad_q.astype(jnp.bfloat16))

    start = (jnp.zeros((N_CTX, BLK, KVH, HD), jnp.float32), jnp.zeros((N_CTX, BLK, KVH, HD), jnp.float32))
    (key_grad_all, value_grad_all), (out_blocks, grad_blocks) = lax.scan(one_block, start, jnp.arange(N_CTX).astype(jnp.int32))
    width = KVH * QPK * HD
    attn_out = out_blocks.reshape(N_CTX * BLK, width)
    grad_query = grad_blocks.reshape(N_CTX * BLK, width)
    grad_key = key_grad_all.astype(jnp.bfloat16).reshape(N_CTX * BLK, KVH * HD)
    grad_value = value_grad_all.astype(jnp.bfloat16).reshape(N_CTX * BLK, KVH * HD)
    return (attn_out, grad_query, grad_key, grad_value)
```

```python
import jax
import jax.numpy as jnp
from jax import lax
from jax.experimental import pallas as pl
from jax.experimental.pallas import tpu as pltpu
from jax.sharding import PartitionSpec as P

HD = 128
LOG2E = 1.4426950408889634
LOW = -1e30

NT = (((1,), (1,)), ((), ()))
NN = (((1,), (0,)), ((), ()))
TN = (((0,), (0,)), ((), ()))


def mm(a, b, dims):
    return lax.dot_general(a, b, dims, preferred_element_type=jnp.float32)


def attention_kernel(levels, peers, group, *refs):
    count = levels * peers
    q_ref, g_ref = refs[:2]
    kv_refs = refs[2 : 2 + count]
    o_ref, dq_ref = refs[2 + count : 4 + count]
    dkv_refs = refs[4 + count :]
    rows = q_ref.shape[0]
    heads = kv_refs[0].shape[1] // (2 * HD)
    width = heads * HD
    wide = group * rows
    scale = HD ** (-0.5)
    factor = scale * LOG2E
    ctx = lax.axis_index("ctx")
    kvh = lax.axis_index("kvh")
    valid = []
    for level in range(levels):
        for j in range(peers):
            if level == 0:
                valid.append(None if j == 0 else lax.bitwise_xor(kvh, j) < kvh)
            else:
                valid.append(ctx >= (1 << (level - 1)))

    def stack(ref, g):
        return jnp.concatenate(
            [ref[:, pl.ds(pl.multiple_of((g * group + r) * HD, HD), HD)] for r in range(group)], axis=0
        )

    def unstack(ref, g, value):
        for r in range(group):
            ref[:, pl.ds(pl.multiple_of((g * group + r) * HD, HD), HD)] = value[r * rows : (r + 1) * rows]

    def head(g, carry):
        queries = stack(q_ref, g)
        grads = stack(g_ref, g)
        at_k = pl.ds(pl.multiple_of(g * HD, HD), HD)
        at_v = pl.ds(pl.multiple_of(g * HD + width, HD), HD)
        keys, values, scores = [], [], []
        top = None
        key_pos = lax.broadcasted_iota(jnp.int32, (rows, wide), 0)
        query_pos = lax.broadcasted_iota(jnp.int32, (rows, wide), 1) % rows
        causal = key_pos <= query_pos
        for level in range(levels):
            part = kv_refs[level * peers : (level + 1) * peers]
            keys.append(jnp.concatenate([ref[:, at_k] for ref in part], axis=0))
            values.append(jnp.concatenate([ref[:, at_v] for ref in part], axis=0))
            raw = mm(keys[level], queries, NT)
            for j in range(peers):
                piece = raw[j * rows : (j + 1) * rows]
                ok = valid[level * peers + j]
                if ok is None:
                    piece = jnp.where(causal, piece, LOW)
                best = jnp.max(piece, axis=0, keepdims=True)
                if ok is not None:
                    best = jnp.where(ok, best, LOW)
                top = best if top is None else jnp.maximum(top, best)
                scores.append(piece)
        top = top * factor
        total = None
        expo = []
        for index in range(levels * peers):
            ok = valid[index]
            shift = top if ok is None else jnp.where(ok, top, -LOW)
            weight = jnp.exp2(scores[index] * factor - shift)
            part = jnp.sum(weight, axis=0, keepdims=True)
            total = part if total is None else total + part
            expo.append(weight)
        inverse = 1.0 / total
        probs, low, out_t = [], [], None
        for level in range(levels):
            prob = jnp.concatenate(expo[level * peers : (level + 1) * peers], axis=0) * inverse
            probs.append(prob)
            low.append(prob.astype(jnp.bfloat16))
            part = mm(values[level], low[level], TN)
            out_t = part if out_t is None else out_t + part
        out = out_t.T.astype(jnp.bfloat16)
        unstack(o_ref, g, out)
        delta = jnp.sum(
            grads.astype(jnp.float32).T * out_t.astype(jnp.bfloat16).astype(jnp.float32), axis=0, keepdims=True
        )
        dq_t = None
        for level in range(levels):
            grad_prob = mm(values[level], grads, NT)
            grad_scores = (probs[level] * (grad_prob - delta)).astype(jnp.bfloat16)
            part = mm(keys[level], grad_scores, TN)
            dq_t = part if dq_t is None else dq_t + part
            grad_k = (mm(grad_scores, queries, NN) * scale).astype(jnp.bfloat16)
            grad_v = mm(low[level], grads, NN).astype(jnp.bfloat16)
            for j in range(peers):
                ref = dkv_refs[level * peers + j]
                ref[:, at_k] = grad_k[j * rows : (j + 1) * rows]
                ref[:, at_v] = grad_v[j * rows : (j + 1) * rows]
        unstack(dq_ref, g, (dq_t * scale).T.astype(jnp.bfloat16))
        return carry

    lax.fori_loop(0, heads, head, 0)


def attention(query, grad, shards, levels, peers):
    rows, q_width = query.shape
    kv_width = shards[0].shape[1]
    group = 2 * q_width // kv_width
    spec = pl.BlockSpec(memory_space=pltpu.VMEM)
    q_shape = jax.ShapeDtypeStruct(query.shape, jnp.bfloat16)
    kv_shape = jax.ShapeDtypeStruct((rows, kv_width), jnp.bfloat16)
    keys = levels * peers * rows
    return pl.pallas_call(
        lambda *refs: attention_kernel(levels, peers, group, *refs),
        out_shape=[q_shape] * 2 + [kv_shape] * (levels * peers),
        in_specs=[spec] * (2 + levels * peers),
        out_specs=[spec] * (2 + levels * peers),
        compiler_params=pltpu.CompilerParams(vmem_limit_bytes=48 * 2**20),
        cost_estimate=pl.CostEstimate(
            flops=12 * rows * q_width * keys, bytes_accessed=8 * rows * q_width, transcendentals=0
        ),
        name="attention",
    )(query, grad, *shards)


AXES = ("ctx", "kvh")


def permute(array, target):
    blocks, peers = lax.axis_size("ctx"), lax.axis_size("kvh")
    pairs = []
    for c in range(blocks):
        for k in range(peers):
            to_c, to_k = target(c, k)
            if 0 <= to_c < blocks:
                pairs.append((c * peers + k, to_c * peers + to_k))
    return lax.ppermute(array, AXES, pairs)


def along(array, by):
    return permute(array, lambda c, k: (c + by, k))


def pair_swap(array):
    return permute(array, lambda c, k: (c ^ 1, k))


def across(array, bit):
    return permute(array, lambda c, k: (c, k ^ bit))


def add(*terms):
    total = terms[0].astype(jnp.float32)
    for term in terms[1:]:
        total = total + term.astype(jnp.float32)
    return total


def low(array):
    return array.astype(jnp.bfloat16)


def shards(query_act, key_act, value_act, grad_out):
    blocks, peers = lax.axis_size("ctx"), lax.axis_size("kvh")
    far = (blocks - 1).bit_length()
    levels = far + 1
    odd = lax.axis_index("ctx") % 2 == 1
    own = jnp.concatenate([key_act, value_act], axis=1)
    held = {(0, 0): own}
    half = peers // 2
    held[2, 0] = along(own, 2)
    held[0, half] = across(own, half)
    held[1, 0] = pair_swap(jnp.where(odd, held[2, 0], own))
    held[2, half] = across(held[2, 0], half)
    for level in range(3, levels):
        held[level, 0] = along(held[level - 1, 0], 1 << (level - 2))
        held[level, half] = along(held[level - 1, half], 1 << (level - 2))
    held[1, half] = across(held[1, 0], half)
    bit = half // 2
    while bit:
        for level in range(levels):
            for j in range(0, peers, 2 * bit):
                held[level, j + bit] = across(held[level, j], bit)
        bit //= 2
    order = [(level, j) for level in range(levels) for j in range(peers)]
    out, grad_query, *parts = attention(query_act, grad_out, [held[at] for at in order], levels, peers)
    sums = dict(zip(order, parts))
    bit = 1
    while bit < half:
        for level in range(levels):
            for j in range(0, peers, 2 * bit):
                sums[level, j] = low(add(sums[level, j], across(sums[level, j + bit], bit)))
        bit *= 2
    for level in range(levels - 1, 2, -1):
        moved = along(sums[level, half], -(1 << (level - 2)))
        sums[level - 1, half] = low(add(sums[level - 1, half], moved))
        moved = along(sums[level, 0], -(1 << (level - 2)))
        sums[level - 1, 0] = low(add(sums[level - 1, 0], moved))
    sums[1, 0] = low(add(sums[1, 0], across(sums[1, half], half)))
    swapped = pair_swap(sums[1, 0])
    nothing = jnp.zeros_like(swapped)
    sums[2, 0] = low(add(sums[2, 0], across(sums[2, half], half), jnp.where(odd, swapped, nothing)))
    total = add(
        sums[0, 0],
        across(sums[0, half], half),
        jnp.where(odd, nothing, swapped),
        along(sums[2, 0], -2),
    )
    total = low(total)
    width = key_act.shape[1]
    return out, grad_query, total[:, :width], total[:, width:]


def solution(mesh):
    spec = P(AXES, None)
    return jax.shard_map(
        shards, mesh=mesh, in_specs=(spec,) * 4, out_specs=(spec,) * 4, check_vma=False
    )
```

```python
import jax
import jax.numpy as jnp
from jax import lax
from jax.experimental import pallas as pl
from jax.experimental.pallas import tpu as pltpu
from jax.sharding import PartitionSpec as P

HD = 128
LOG2E = 1.4426950408889634
LOW = -1e30

NT = (((1,), (1,)), ((), ()))
NN = (((1,), (0,)), ((), ()))
TN = (((0,), (0,)), ((), ()))


def mm(a, b, dims):
    return lax.dot_general(a, b, dims, preferred_element_type=jnp.float32)


def attention_kernel(levels, peers, group, per, homes, *refs):
    count = levels * peers
    q_ref, g_ref = refs[:2]
    kv_refs = refs[2 : 2 + count]
    o_ref, dq_ref = refs[2 + count : 4 + count]
    dkv_refs = refs[4 + count :]
    homes = {at: (dkv_refs[place], pl.ds(index * q_ref.shape[0], q_ref.shape[0])) for at, (place, index) in homes.items()}
    rows = q_ref.shape[0]
    width = kv_refs[0].shape[1] // 2
    wide = group * rows
    scale = HD ** (-0.5)
    factor = scale * LOG2E
    ctx = lax.axis_index("ctx")
    kvh = lax.axis_index("kvh")
    key_pos = lax.broadcasted_iota(jnp.int32, (rows, wide), 0)
    query_pos = lax.broadcasted_iota(jnp.int32, (rows, wide), 1) % rows
    causal = key_pos <= query_pos

    def counts(level, j):
        if level == 0:
            return lax.bitwise_xor(kvh, j) < kvh
        return ctx >= (1 << (level - 1))

    class Head:
        def __init__(self, index):
            self.first = index * group * HD
            self.head = pl.program_id(0) * per + index
            self.at_k = pl.ds(pl.multiple_of(self.head * HD, HD), HD)
            self.at_v = pl.ds(pl.multiple_of(self.head * HD + width, HD), HD)

        def stack(self, ref):
            return jnp.concatenate(
                [ref[:, self.first + r * HD : self.first + (r + 1) * HD] for r in range(group)], axis=0
            )

        def unstack(self, ref, value):
            for r in range(group):
                ref[:, self.first + r * HD : self.first + (r + 1) * HD] = value[r * rows : (r + 1) * rows]

        def keys(self, level):
            return jnp.concatenate([ref[:, self.at_k] for ref in kv_refs[level * peers : (level + 1) * peers]], axis=0)

        def values(self, level):
            return jnp.concatenate([ref[:, self.at_v] for ref in kv_refs[level * peers : (level + 1) * peers]], axis=0)

        def start(self):
            self.queries = self.stack(q_ref)
            self.grads = self.stack(g_ref)
            self.queries_t, self.grads_t = self.queries.T, self.grads.T
            self.top, self.total, self.out_t, self.dq_t = None, None, None, None
            self.scores, self.weights, self.grad_prob = [], [], []

        def score(self, level):
            raw = mm(self.keys(level), self.queries_t, NN)
            for j in range(peers):
                piece = raw[j * rows : (j + 1) * rows]
                if level == 0 and j == 0:
                    piece = jnp.where(causal, piece, LOW)
                best = jnp.max(piece, axis=0, keepdims=True)
                if level or j:
                    best = jnp.where(counts(level, j), best, LOW)
                self.top = best if self.top is None else jnp.maximum(self.top, best)
                self.scores.append(piece)

        def weigh(self, level):
            top = self.top * factor
            pieces = []
            for j in range(peers):
                shift = jnp.where(counts(level, j), top, -LOW) if level or j else top
                weight = jnp.exp2(self.scores[level * peers + j] * factor - shift)
                part = jnp.sum(weight, axis=0, keepdims=True)
                self.total = part if self.total is None else self.total + part
                pieces.append(weight.astype(jnp.bfloat16))
            self.weights.append(jnp.concatenate(pieces, axis=0))
            part = mm(self.values(level), self.weights[level], TN)
            self.out_t = part if self.out_t is None else self.out_t + part

        def finish(self):
            self.inverse = 1.0 / self.total
            out_t = (self.out_t * self.inverse).astype(jnp.bfloat16)
            self.unstack(o_ref, out_t.T)
            self.delta = jnp.sum(
                self.grads_t.astype(jnp.float32) * out_t.astype(jnp.float32), axis=0, keepdims=True
            )
            spread = jnp.broadcast_to(self.inverse, (HD, wide)).T
            self.queries_low = (self.queries.astype(jnp.float32) * (spread * scale)).astype(jnp.bfloat16)
            self.grads_low = (self.grads.astype(jnp.float32) * spread).astype(jnp.bfloat16)

        def back(self, level):
            grad_prob = mm(self.values(level), self.grads_t, NN) - self.delta
            grad_scores = self.weights[level] * grad_prob.astype(jnp.bfloat16)
            part = mm(self.keys(level), grad_scores, TN)
            self.dq_t = part if self.dq_t is None else self.dq_t + part
            grad_k = mm(grad_scores, self.queries_low, NN).astype(jnp.bfloat16)
            grad_v = mm(self.weights[level], self.grads_low, NN).astype(jnp.bfloat16)
            for j in range(peers):
                ref, at = homes[level, j]
                ref[at, self.at_k] = grad_k[j * rows : (j + 1) * rows]
                ref[at, self.at_v] = grad_v[j * rows : (j + 1) * rows]

        def end(self):
            self.unstack(dq_ref, (self.dq_t * (self.inverse * scale)).T.astype(jnp.bfloat16))

    heads = [Head(index) for index in range(per)]
    first = heads[0]
    first.start()
    for level in range(levels):
        first.score(level)
    for index, head in enumerate(heads):
        after = heads[index + 1] if index + 1 < per else None
        if after:
            after.start()
        for level in range(levels):
            head.weigh(level)
            if after:
                after.score(level)
        head.finish()
        for level in range(levels):
            head.back(level)
        head.end()


def attention(query, grad, shards, levels, peers, parts):
    rows, q_width = query.shape
    kv_width = shards[0].shape[1]
    heads = kv_width // (2 * HD)
    group = q_width // (heads * HD)
    per = 4
    whole = pl.BlockSpec(memory_space=pltpu.VMEM)
    block = pl.BlockSpec((rows, per * group * HD), lambda step: (0, step))
    q_shape = jax.ShapeDtypeStruct(query.shape, jnp.bfloat16)
    kv_shapes = [jax.ShapeDtypeStruct((rows * len(part), kv_width), jnp.bfloat16) for part in parts]
    homes = {at: (place, index) for place, part in enumerate(parts) for index, at in enumerate(part)}
    count = levels * peers
    return pl.pallas_call(
        lambda *refs: attention_kernel(levels, peers, group, per, homes, *refs),
        grid=(heads // per,),
        out_shape=[q_shape] * 2 + kv_shapes,
        in_specs=[block] * 2 + [whole] * count,
        out_specs=[block] * 2 + [whole] * len(parts),
        compiler_params=pltpu.CompilerParams(vmem_limit_bytes=32 * 2**20),
        cost_estimate=pl.CostEstimate(
            flops=12 * rows * q_width * count * rows, bytes_accessed=8 * rows * q_width, transcendentals=0
        ),
        name="attention",
    )(query, grad, *shards)


def merge(body, inputs, shapes, name):
    def kernel(*refs):
        body(refs[: len(inputs)], refs[len(inputs) :])

    whole = pl.BlockSpec(memory_space=pltpu.VMEM)
    return pl.pallas_call(
        kernel,
        out_shape=[jax.ShapeDtypeStruct(shape, jnp.bfloat16) for shape in shapes],
        in_specs=[whole] * len(inputs),
        out_specs=[whole] * len(shapes),
        compiler_params=pltpu.CompilerParams(vmem_limit_bytes=12 * 2**20),
        name=name,
    )(*inputs)


AXES = ("ctx", "kvh")


def permute(array, target):
    blocks, peers = lax.axis_size("ctx"), lax.axis_size("kvh")
    pairs = []
    for c in range(blocks):
        for k in range(peers):
            to_c, to_k = target(c, k)
            pairs.append((c * peers + k, to_c % blocks * peers + to_k))
    return lax.ppermute(array, AXES, pairs)


def along(array, by):
    return permute(array, lambda c, k: (c + by, k))


def pair_swap(array):
    return permute(array, lambda c, k: (c ^ 1, k))


def across(array):
    return permute(array, lambda c, k: (c, k ^ 2))


def sibling(array):
    return permute(array, lambda c, k: (c, k ^ 1))


def wide(value):
    return value.astype(jnp.float32)


def low(value):
    return value.astype(jnp.bfloat16)


def gather(own, levels, odd):
    held = {(0, 0): own}
    held[2, 0] = along(own, 2)
    held[0, 2] = across(own)
    held[0, 1] = sibling(own)
    for level in range(3, levels):
        held[level, 0] = along(held[level - 1, 0], 1 << (level - 2))
    held[2, 2] = across(held[2, 0])
    held[1, 0] = pair_swap(jnp.where(odd, held[2, 0], own))
    held[0, 3] = sibling(held[0, 2])
    held[2, 1] = sibling(held[2, 0])
    for level in range(3, levels):
        held[level, 2] = across(held[level, 0])
    held[1, 2] = pair_swap(jnp.where(odd, held[2, 2], held[0, 2]))
    held[2, 3] = sibling(held[2, 2])
    held[1, 1] = sibling(held[1, 0])
    held[1, 3] = sibling(held[1, 2])
    for level in range(3, levels):
        held[level, 1] = sibling(held[level, 0])
        held[level, 3] = sibling(held[level, 2])
    return held


def scatter(parts, levels, rows, width):
    keep_a, keep_b, keep_c, send_a, send_b, send_c = parts
    tall = 2 * width
    shape = (rows, tall)
    far = levels - 1

    def at(ref, index):
        return wide(ref[index * rows : (index + 1) * rows])

    def is_odd():
        return lax.axis_index("ctx") % 2 == 1

    got_a = sibling(send_a)
    got_b = sibling(send_b)
    got_c = sibling(send_c)

    def first(ins, outs):
        keep, got = ins
        for index, out in enumerate(outs):
            out[...] = low(at(keep, index) + at(got, index))

    *far_2, near_2 = merge(first, [keep_a, got_a], [shape] * (far - 1), "first")
    got_far = [across(array) for array in far_2]
    got_near = pair_swap(near_2)

    def second(ins, outs):
        keep, got, swapped, *crossed = ins
        from_pair = wide(swapped[...])
        odd = is_odd()
        none = jnp.zeros_like(from_pair)
        outs[0][...] = low(at(keep, 0) + at(got, 0) + jnp.where(odd, from_pair, none))
        outs[1][...] = low(at(keep, 1) + at(got, 1) + jnp.where(odd, none, from_pair))
        outs[2][...] = low(at(keep, 2) + at(got, 2))
        for index, other in enumerate(crossed):
            outs[3 + index][...] = low(at(keep, 3 + index) + at(got, 3 + index) + wide(other[...]))

    two_2, zero_2, one_0, *far_0 = merge(
        second, [keep_b, got_b, got_near] + got_far, [shape] * (far + 1), "second"
    )
    chain = far_0[-1]
    for level in range(far, 3, -1):
        chain = low(wide(far_0[level - 4]) + wide(along(chain, -(1 << (level - 2)))))
    got_chain = along(chain, -2)
    got_two = across(two_2)
    got_one = pair_swap(one_0)

    def third(ins, outs):
        keep, got, chain, two, one = ins
        from_pair = wide(one[...])
        terms = jnp.where(is_odd(), from_pair, jnp.zeros_like(from_pair))
        outs[0][...] = low(at(keep, 0) + at(got, 0) + wide(chain[...]) + wide(two[...]) + terms)

    (two_0,) = merge(third, [keep_c, got_c, got_chain, got_two, got_one], [shape], "third")
    got_chain = along(two_0, -2)
    got_zero = across(zero_2)

    def fourth(ins, outs):
        keep, got, one, zero, chain = ins
        from_pair = wide(one[...])
        terms = jnp.where(is_odd(), jnp.zeros_like(from_pair), from_pair)
        total = at(keep, 1) + at(got, 1) + wide(chain[...]) + wide(zero[...]) + terms
        outs[0][...] = low(total[:, :width])
        outs[1][...] = low(total[:, width:])

    return merge(fourth, [keep_c, got_c, got_one, got_zero, got_chain], [(rows, width)] * 2, "fourth")


def shards(query_act, key_act, value_act, grad_out):
    blocks, peers = lax.axis_size("ctx"), lax.axis_size("kvh")
    levels = (blocks - 1).bit_length() + 1
    odd = lax.axis_index("ctx") % 2 == 1
    rows, width = key_act.shape

    def join(ins, outs):
        outs[0][:, :width] = ins[0][...]
        outs[0][:, width:] = ins[1][...]

    (own,) = merge(join, [key_act, value_act], [(rows, 2 * width)], "join")
    held = gather(own, levels, odd)
    ordered = [held[level, j] for level in range(levels) for j in range(peers)]
    later = list(range(3, levels))
    kept = [
        [(level, 2) for level in later] + [(1, 2)],
        [(2, 2), (0, 2), (1, 0)] + [(level, 0) for level in later],
        [(2, 0), (0, 0)],
    ]
    sent = [[(level, j + 1) for level, j in part] for part in kept]
    out, grad_query, *parts = attention(query_act, grad_out, ordered, levels, peers, kept + sent)
    grad_key, grad_value = scatter(parts, levels, rows, width)
    return out, grad_query, grad_key, grad_value


def solution(mesh):
    spec = P(AXES, None)
    return jax.shard_map(
        shards, mesh=mesh, in_specs=(spec,) * 4, out_specs=(spec,) * 4, check_vma=False
    )
```

```python
import jax
import jax.numpy as jnp
from jax import lax
from jax.experimental import pallas as pl
from jax.experimental.pallas import tpu as pltpu
from jax.sharding import PartitionSpec as P

HD = 128
LOG2E = 1.4426950408889634
LOW = -1e30

NN = (((1,), (0,)), ((), ()))
TN = (((0,), (0,)), ((), ()))

MIB = 2**20
AXES = ("ctx", "kvh")
WHOLE = pl.BlockSpec(memory_space=pltpu.VMEM)
HBM = pl.BlockSpec(memory_space=pltpu.HBM)


def mm(a, b, dims):
    return lax.dot_general(a, b, dims, preferred_element_type=jnp.float32)


def wide(value):
    return value.astype(jnp.float32)


def low(value):
    return value.astype(jnp.bfloat16)


def like(shape, dtype=jnp.bfloat16):
    return jax.ShapeDtypeStruct(shape, dtype)


def is_odd():
    return lax.axis_index("ctx") % 2 == 1


class Head:
    def __init__(self, index, per, group, width):
        self.index = index
        self.number = pl.program_id(0) * per + index
        self.group = group
        self.first = self.number * group * HD
        self.at_k = pl.ds(pl.multiple_of(self.number * HD, HD), HD)
        self.at_v = pl.ds(pl.multiple_of(self.number * HD + width, HD), HD)

    def column(self, r):
        return pl.ds(pl.multiple_of(self.first + r * HD, HD), HD)

    def keys(self, shards):
        return jnp.concatenate([ref[:, self.at_k] for ref in shards], axis=0)

    def values(self, shards):
        return jnp.concatenate([ref[:, self.at_v] for ref in shards], axis=0)

    def stack(self, mine, other, at):
        base = self.index * self.group
        blocks = [mine[:, (base + r) * HD : (base + r + 1) * HD] for r in range(self.group)]
        blocks += [other[at, r * HD : (r + 1) * HD] for r in range(self.group)]
        return jnp.concatenate(blocks, axis=0)

    def unstack(self, refs, value):
        rows = refs[0].shape[0]
        for side, ref in enumerate(refs):
            for r in range(self.group):
                at = (side * self.group + r) * rows
                ref[:, self.column(r)] = value[at : at + rows]

    def back(self, shards, weights, grads_t, delta, queries_low, grads_low, homes):
        rows = shards[0].shape[0]
        grad_prob = mm(self.values(shards), grads_t, NN) - delta
        grad_scores = weights * low(grad_prob)
        term = mm(self.keys(shards), grad_scores, TN)
        grad_k = low(mm(grad_scores, queries_low, NN))
        grad_v = low(mm(weights, grads_low, NN))
        for index, ref in enumerate(homes):
            part = slice(index * rows, (index + 1) * rows)
            ref[:, self.at_k] = grad_k[part]
            ref[:, self.at_v] = grad_v[part]
        return term


def split(refs, groups):
    parts = []
    for part in groups:
        parts.append(refs[: len(part)])
        refs = refs[len(part) :]
    return parts, refs


def forward_kernel(groups, group, per, *refs):
    q_ref, g_ref = refs[:2]
    others, refs = refs[2 : 2 + per], refs[2 + per :]
    shards, refs = split(refs, groups)
    outs, refs = refs[:2], refs[2:]
    homes, refs = refs[: len(groups[0])], refs[len(groups[0]) :]
    weight_refs, refs = refs[: len(groups) - 1], refs[len(groups) - 1 :]
    gt_ref, ql_ref, gl_ref, delta_ref, factor_ref, dq_ref = refs
    rows = q_ref.shape[0]
    width = shards[0][0].shape[1] // 2
    half = group * rows
    span = 2 * half
    scale = HD ** (-0.5)
    factor = scale * LOG2E
    ctx = lax.axis_index("ctx")
    kvh = lax.axis_index("kvh")
    key_pos = lax.broadcasted_iota(jnp.int32, (rows, span), 0)
    column = lax.broadcasted_iota(jnp.int32, (rows, span), 1)
    causal = key_pos <= column % rows
    own = lax.broadcasted_iota(jnp.int32, (1, span), 1) < half
    diagonal = [causal | (column >= half), causal | (column < half)]

    def choose(level, hi, j, value, other):
        if level:
            return jnp.where(ctx >= (1 << (level - 1)), value, other)
        sides = []
        for i in range(2):
            if hi == 0 and i == j:
                sides.append(value)
            else:
                before = lax.bitwise_xor(kvh, hi ^ j) < lax.bitwise_xor(kvh, i)
                sides.append(jnp.where(before, value, other))
        return jnp.where(own, sides[0], sides[1])

    class Forward(Head):
        def start(self):
            self.queries = self.stack(q_ref, others[self.index], slice(0, rows))
            self.grads = self.stack(g_ref, others[self.index], slice(rows, 2 * rows))
            self.queries_t, self.grads_t = self.queries.T, self.grads.T
            self.top, self.total, self.out_t = None, None, None
            self.scores, self.weights = [], []

        def score(self, place):
            raw = mm(self.keys(shards[place]), self.queries_t, NN)
            pieces = []
            for index, (level, hi) in enumerate(groups[place]):
                for j in range(2):
                    at = (2 * index + j) * rows
                    piece = raw[at : at + rows]
                    if level == 0 and hi == 0:
                        piece = jnp.where(diagonal[j], piece, LOW)
                    best = choose(level, hi, j, jnp.max(piece, axis=0, keepdims=True), LOW)
                    self.top = best if self.top is None else jnp.maximum(self.top, best)
                    pieces.append(piece)
            self.scores.append(pieces)

        def weigh(self, place):
            top = self.top * factor
            pieces = []
            for index, (level, hi) in enumerate(groups[place]):
                for j in range(2):
                    shift = choose(level, hi, j, top, -LOW)
                    weight = jnp.exp2(self.scores[place][2 * index + j] * factor - shift)
                    part = jnp.sum(weight, axis=0, keepdims=True)
                    self.total = part if self.total is None else self.total + part
                    pieces.append(low(weight))
            weights = jnp.concatenate(pieces, axis=0)
            self.weights.append(weights)
            if place:
                weight_refs[place - 1][self.number] = weights
            part = mm(self.values(shards[place]), weights, TN)
            self.out_t = part if self.out_t is None else self.out_t + part

        def finish(self):
            inverse = 1.0 / self.total
            out_t = low(self.out_t * inverse)
            self.unstack(outs, out_t.T)
            delta = jnp.sum(wide(self.grads_t) * wide(out_t), axis=0, keepdims=True)
            spread = jnp.broadcast_to(inverse, (HD, span)).T
            queries_low = low(wide(self.queries) * (spread * scale))
            grads_low = low(wide(self.grads) * spread)
            gt_ref[self.number] = self.grads_t
            ql_ref[self.number] = queries_low
            gl_ref[self.number] = grads_low
            delta_ref[self.number] = delta
            factor_ref[self.number] = inverse * scale
            dq_ref[self.number] = self.back(
                shards[0], self.weights[0], self.grads_t, delta, queries_low, grads_low, homes
            )

    heads = [Forward(index, per, group, width) for index in range(per)]
    places = range(len(groups))
    heads[0].start()
    for place in places:
        heads[0].score(place)
    for index, head in enumerate(heads):
        after = heads[index + 1] if index + 1 < per else None
        if after:
            after.start()
        for place in places:
            head.weigh(place)
            if after:
                after.score(place)
        head.finish()


def backward_kernel(groups, group, per, last, *refs):
    shards, refs = split(refs, groups)
    weight_refs, refs = refs[: len(groups)], refs[len(groups) :]
    gt_ref, ql_ref, gl_ref, delta_ref, factor_ref, dq_ref, *refs = refs
    dq_outs, refs = (refs[:2], refs[2:]) if last else (refs[:1], refs[1:])
    homes, refs = split(refs, groups)
    width = shards[0][0].shape[1] // 2
    for index in range(per):
        head = Head(index, per, group, width)
        at = head.number
        term = dq_ref[at]
        for place in range(len(groups)):
            term = term + head.back(
                shards[place],
                weight_refs[place][at],
                gt_ref[at],
                delta_ref[at],
                ql_ref[at],
                gl_ref[at],
                homes[place],
            )
        if last:
            head.unstack(dq_outs, low(term * factor_ref[at]).T)
        else:
            dq_outs[0][at] = term


def call(kernel, inputs, shapes, name, limit=12, grid=(), cost=None, in_spec=WHOLE, out_spec=WHOLE, scratch=()):
    return pl.pallas_call(
        kernel,
        grid=grid,
        out_shape=shapes,
        in_specs=in_spec if isinstance(in_spec, list) else [in_spec] * len(inputs),
        out_specs=[out_spec] * len(shapes),
        scratch_shapes=scratch,
        compiler_params=pltpu.CompilerParams(vmem_limit_bytes=limit * MIB),
        cost_estimate=cost,
        name=name,
    )(*inputs)


FREE = pl.CostEstimate(flops=0, bytes_accessed=0, transcendentals=0)


def merge(body, inputs, shapes, name):
    def kernel(*refs):
        body(refs[: len(inputs)], refs[len(inputs) :])

    return call(kernel, inputs, [like(shape) for shape in shapes], name)


def cost(keys, span, heads, matmuls):
    return pl.CostEstimate(flops=2 * keys * span * HD * heads * matmuls, bytes_accessed=0, transcendentals=0)


def sizes(others):
    return others[0].shape[0] // 2, len(others), others[0].shape[1] // HD


def forward(query, grad, others, held, groups):
    rows, heads, group = sizes(others)
    span = 2 * group * rows
    shards = [held[at] for part in groups for at in part]
    keys = shards[0].shape[0]
    per = heads
    steps = heads // per
    block = pl.BlockSpec((rows, per * group * HD), lambda step: (0, side() * steps + step))
    shapes = [like((rows, heads * group * HD))] * 2
    shapes += [like(shards[0].shape)] * len(groups[0])
    shapes += [like((heads, len(part) * keys, span)) for part in groups[1:]]
    shapes += [like((heads, HD, span)), like((heads, span, HD)), like((heads, span, HD))]
    shapes += [like((heads, 1, span), jnp.float32)] * 2 + [like((heads, HD, span), jnp.float32)]
    rest = call(
        lambda *refs: forward_kernel(groups, group, per, *refs),
        [query, grad, *others] + shards,
        shapes,
        "forward",
        limit=28,
        grid=(steps,),
        cost=cost(keys, span, heads, 2 * len(shards) + 4 * len(groups[0])),
        in_spec=[block] * 2 + [WHOLE] * (heads + len(shards)),
    )
    outs, rest = rest[:2], rest[2:]
    sums, rest = rest[: len(groups[0])], rest[len(groups[0]) :]
    return outs, sums, list(rest[: len(groups) - 1]), list(rest[len(groups) - 1 :])


def backward(others, held, groups, weights, state, last, after=()):
    rows, heads, group = sizes(others)
    span = 2 * group * rows
    shards = [held[at] for part in groups for at in part]
    keys = shards[0].shape[0]
    per = 2
    shapes = [like((rows, heads * group * HD))] * 2 if last else [like(state[-1].shape, state[-1].dtype)]
    heading = len(shapes)
    shapes += [like(shards[0].shape)] * len(shards)
    result = call(
        lambda *refs: backward_kernel(groups, group, per, last, *refs[len(after) :]),
        list(after) + shards + list(weights) + list(state),
        shapes,
        "backward",
        limit=14,
        grid=(heads // per,),
        cost=cost(keys, span, heads, 4 * len(shards)),
    )
    sums = dict(zip([at for part in groups for at in part], result[heading:]))
    return result[:heading], sums


def side():
    return lax.axis_index("kvh") % 2


def halves(array, place):
    rows, width = array.shape
    return pl.BlockSpec((rows, width // 2), lambda step: (0, side() ^ place))


def deal(key, value):
    rows, width = key.shape
    half = width // 2

    def kernel(key_kept, value_kept, key_sent, value_sent, kept, sent):
        kept[:, :half] = key_kept[...]
        kept[:, half:] = value_kept[...]
        sent[:, :half] = key_sent[...]
        sent[:, half:] = value_sent[...]

    specs = [halves(array, place) for place in range(2) for array in (key, value)]
    return call(kernel, [key, value] * 2, [like((rows, width))] * 2, "deal", grid=(1,), in_spec=specs, cost=FREE)


def pack(query, grad, after, heads):
    rows, width = query.shape
    share = width // 2 // heads

    def kernel(query_ref, grad_ref, after_ref, *outs):
        for index, out in enumerate(outs):
            out[:rows] = query_ref[:, index * share : (index + 1) * share]
            out[rows:] = grad_ref[:, index * share : (index + 1) * share]

    specs = [halves(query, 1), halves(grad, 1), WHOLE]
    shapes = [like((2 * rows, share))] * heads
    return call(kernel, [query, grad, after], shapes, "pack", grid=(1,), in_spec=specs, cost=FREE)


def assemble(pairs):
    rows, half = pairs[0][0].shape
    inputs = [array for pair in pairs for array in pair]

    def kernel(*refs):
        outs, sems = refs[len(inputs) : -1], refs[-1]
        copies = []
        for index, ref in enumerate(refs[: len(inputs)]):
            start = pl.multiple_of((side() ^ (index % 2)) * half, half)
            target = outs[index // 2].at[:, pl.ds(start, half)]
            copies.append(pltpu.make_async_copy(ref, target, sems.at[index]))
        for copy in copies:
            copy.start()
        for copy in copies:
            copy.wait()

    return call(
        kernel,
        inputs,
        [like((rows, 2 * half))] * len(pairs),
        "assemble",
        out_spec=HBM,
        scratch=[pltpu.SemaphoreType.DMA((len(inputs),))],
    )


def permute(array, target):
    blocks, peers = lax.axis_size("ctx"), lax.axis_size("kvh")
    pairs = []
    for c in range(blocks):
        for k in range(peers):
            to_c, to_k = target(c, k)
            pairs.append((c * peers + k, to_c % blocks * peers + to_k))
    return lax.ppermute(array, AXES, pairs)


def along(array, by):
    return permute(array, lambda c, k: (c + by, k))


def pair_swap(array):
    return permute(array, lambda c, k: (c ^ 1, k))


def across(array):
    return permute(array, lambda c, k: (c, k ^ 2))


def sibling(array):
    return permute(array, lambda c, k: (c, k ^ 1))


def gather(own, levels):
    odd = is_odd()
    held = {(0, 0): own}
    held[2, 0] = along(own, 2)
    held[0, 2] = across(own)
    for level in range(3, levels):
        held[level, 0] = along(held[level - 1, 0], 1 << (level - 2))
    held[2, 2] = across(held[2, 0])
    held[1, 0] = pair_swap(jnp.where(odd, held[2, 0], own))
    for level in range(3, levels):
        held[level, 2] = across(held[level, 0])
    held[1, 2] = pair_swap(jnp.where(odd, held[2, 2], held[0, 2]))
    return held


def shards(query_act, key_act, value_act, grad_out):
    blocks, peers = lax.axis_size("ctx"), lax.axis_size("kvh")
    assert peers == 4, peers
    levels = (blocks - 1).bit_length() + 1
    later = range(3, levels)
    rows, width = key_act.shape
    shape = (2 * rows, width)

    kept, sent = deal(key_act, value_act)

    def stack(ins, outs):
        outs[0][:rows] = ins[0][...]
        outs[0][rows:] = ins[1][...]

    (own,) = merge(stack, [kept, sibling(sent)], [shape], "stack")
    held = gather(own, levels)
    heads = width // (2 * HD)
    others = [sibling(array) for array in pack(query_act, grad_out, held[0, 2], heads)]

    group_a = [(level, 2) for level in later] + [(1, 2)]
    group_b = [(2, 2), (0, 2)]
    group_c = [(level, 0) for level in later] + [(1, 0)]
    group_d = [(2, 0), (0, 0)]
    outs, sums_a, weights, state = forward(query_act, grad_out, others, held, [group_a, group_b, group_c, group_d])
    *far_2, near_2 = sums_a
    got_far = [across(array) for array in far_2]
    got_near = pair_swap(near_2)
    (dq_t,), sums = backward(others, held, [group_b, group_c], weights[:2], state, False)
    got_out = sibling(outs[1])

    def second(ins, outs):
        two, zero, swapped, *rest = ins
        from_pair = wide(swapped[...])
        odd = is_odd()
        none = jnp.zeros_like(from_pair)
        outs[0][...] = low(wide(two[...]) + jnp.where(odd, from_pair, none))
        outs[1][...] = low(wide(zero[...]) + jnp.where(odd, none, from_pair))
        for index in range(len(later)):
            outs[2 + index][...] = low(wide(rest[2 * index][...]) + wide(rest[2 * index + 1][...]))

    far_0 = [array for pair in zip([sums[level, 0] for level in later], got_far) for array in pair]
    two_2, zero_2, *far_0 = merge(
        second, [sums[2, 2], sums[0, 2], got_near] + far_0, [shape] * (len(later) + 2), "second"
    )
    chain = far_0[-1]
    for level in range(levels - 1, 3, -1):
        chain = low(wide(far_0[level - 4]) + wide(along(chain, -(1 << (level - 2)))))
    got_chain = along(chain, -2)
    got_two = across(two_2)
    got_one = pair_swap(sums[1, 0])
    dqs, last_sums = backward(others, held, [group_d], weights[2:], state[:-1] + [dq_t], True, [two_2])
    got_dq = sibling(dqs[1])

    def third(ins, outs):
        base, chain, two, one = ins
        from_pair = wide(one[...])
        terms = jnp.where(is_odd(), from_pair, jnp.zeros_like(from_pair))
        outs[0][...] = low(wide(base[...]) + wide(chain[...]) + wide(two[...]) + terms)

    (two_0,) = merge(third, [last_sums[2, 0], got_chain, got_two, got_one], [shape], "third")
    got_chain = along(two_0, -2)
    got_zero = across(zero_2)
    out, grad_query = assemble([(outs[0], got_out), (dqs[0], got_dq)])

    def fourth(ins, outs):
        base, one, zero, chain = ins[:4]
        from_pair = wide(one[...])
        terms = jnp.where(is_odd(), jnp.zeros_like(from_pair), from_pair)
        total = low(wide(base[...]) + wide(chain[...]) + wide(zero[...]) + terms)
        outs[0][...] = total[:rows]
        outs[1][...] = total[rows:]

    kept, sent = merge(
        fourth,
        [last_sums[0, 0], got_one, got_zero, got_chain],
        [(rows, width)] * 2,
        "fourth",
    )

    def fifth(ins, outs):
        half = width // 2
        for place, ref in enumerate(ins):
            at = pl.ds(pl.multiple_of((side() ^ place) * half, half), half)
            outs[0][:, at] = ref[:, :half]
            outs[1][:, at] = ref[:, half:]

    grad_key, grad_value = merge(fifth, [kept, sibling(sent)], [(rows, width)] * 2, "fifth")
    return out, grad_query, grad_key, grad_value


def solution(mesh):
    spec = P(AXES, None)
    return jax.shard_map(
        shards, mesh=mesh, in_specs=(spec,) * 4, out_specs=(spec,) * 4, check_vma=False
    )
```

```python
import jax
import jax.numpy as jnp
from jax import lax
from jax.experimental import pallas as pl
from jax.experimental.pallas import tpu as pltpu
from jax.sharding import PartitionSpec as P

HD = 128
LOG2E = 1.4426950408889634
LOW = -1e30

NN = (((1,), (0,)), ((), ()))
TN = (((0,), (0,)), ((), ()))

MIB = 2**20
AXES = ("ctx", "kvh")
WHOLE = pl.BlockSpec(memory_space=pltpu.VMEM)
HBM = pl.BlockSpec(memory_space=pltpu.HBM)


def mm(a, b, dims):
    return lax.dot_general(a, b, dims, preferred_element_type=jnp.float32)


def wide(value):
    return value.astype(jnp.float32)


def low(value):
    return value.astype(jnp.bfloat16)


def like(shape, dtype=jnp.bfloat16):
    return jax.ShapeDtypeStruct(shape, dtype)


def is_odd():
    return lax.axis_index("ctx") % 2 == 1


class Head:
    def __init__(self, index, per, group, width):
        self.index = index
        self.number = pl.program_id(0) * per + index
        self.group = group
        self.first = self.number * group * HD
        self.at_k = pl.ds(pl.multiple_of(self.number * HD, HD), HD)
        self.at_v = pl.ds(pl.multiple_of(self.number * HD + width, HD), HD)

    def column(self, r):
        return pl.ds(pl.multiple_of(self.first + r * HD, HD), HD)

    def keys(self, shards):
        return jnp.concatenate([ref[:, self.at_k] for ref in shards], axis=0)

    def values(self, shards):
        return jnp.concatenate([ref[:, self.at_v] for ref in shards], axis=0)

    def stack(self, mine, other, at):
        base = self.index * self.group
        blocks = [mine[:, (base + r) * HD : (base + r + 1) * HD] for r in range(self.group)]
        blocks += [other[at, r * HD : (r + 1) * HD] for r in range(self.group)]
        return jnp.concatenate(blocks, axis=0)

    def unstack(self, refs, value):
        rows = refs[0].shape[0]
        for side, ref in enumerate(refs):
            for r in range(self.group):
                at = (side * self.group + r) * rows
                ref[:, self.column(r)] = value[at : at + rows]

    def back(self, shards, weights, grads_t, delta, queries_low, grads_low, homes):
        rows = shards[0].shape[0]
        grad_prob = mm(self.values(shards), grads_t, NN) - delta
        grad_scores = weights * low(grad_prob)
        term = mm(self.keys(shards), grad_scores, TN)
        grad_k = low(mm(grad_scores, queries_low, NN))
        grad_v = low(mm(weights, grads_low, NN))
        for index, ref in enumerate(homes):
            part = slice(index * rows, (index + 1) * rows)
            ref[:, self.at_k] = grad_k[part]
            ref[:, self.at_v] = grad_v[part]
        return term


def split(refs, groups):
    parts = []
    for part in groups:
        parts.append(refs[: len(part)])
        refs = refs[len(part) :]
    return parts, refs


def forward_kernel(groups, group, per, *refs):
    q_ref, g_ref = refs[:2]
    others, refs = refs[2 : 2 + per], refs[2 + per :]
    shards, refs = split(refs, groups)
    outs, refs = refs[:2], refs[2:]
    homes, refs = refs[: len(groups[0])], refs[len(groups[0]) :]
    weight_refs, refs = refs[: len(groups) - 1], refs[len(groups) - 1 :]
    gt_ref, ql_ref, gl_ref, delta_ref, factor_ref, dq_ref = refs
    rows = q_ref.shape[0]
    width = shards[0][0].shape[1] // 2
    half = group * rows
    span = 2 * half
    scale = HD ** (-0.5)
    factor = scale * LOG2E
    ctx = lax.axis_index("ctx")
    kvh = lax.axis_index("kvh")
    key_pos = lax.broadcasted_iota(jnp.int32, (rows, span), 0)
    column = lax.broadcasted_iota(jnp.int32, (rows, span), 1)
    causal = key_pos <= column % rows
    own = lax.broadcasted_iota(jnp.int32, (1, span), 1) < half
    diagonal = [causal | (column >= half), causal | (column < half)]

    def choose(level, hi, j, value, other):
        if level:
            return jnp.where(ctx >= (1 << (level - 1)), value, other)
        sides = []
        for i in range(2):
            if hi == 0 and i == j:
                sides.append(value)
            else:
                before = lax.bitwise_xor(kvh, hi ^ j) < lax.bitwise_xor(kvh, i)
                sides.append(jnp.where(before, value, other))
        return jnp.where(own, sides[0], sides[1])

    class Forward(Head):
        def start(self):
            self.queries = self.stack(q_ref, others[self.index], slice(0, rows))
            self.grads = self.stack(g_ref, others[self.index], slice(rows, 2 * rows))
            self.queries_t, self.grads_t = self.queries.T, self.grads.T
            self.top, self.total, self.out_t = None, None, None
            self.scores, self.weights = [], []

        def score(self):
            used = [shards[place][index] for place in places for index in active[place]]
            raw = mm(self.keys(used), self.queries_t, NN)
            at = 0
            for place in places:
                pieces = []
                for index in active[place]:
                    level, hi = groups[place][index]
                    for j in range(2):
                        piece = raw[at : at + rows]
                        at += rows
                        if level == 0 and hi == 0:
                            piece = jnp.where(diagonal[j], piece, LOW)
                        best = choose(level, hi, j, jnp.max(piece, axis=0, keepdims=True), LOW)
                        self.top = best if self.top is None else jnp.maximum(self.top, best)
                        pieces.append(piece)
                self.scores.append(pieces)

        def weigh(self, place):
            top = self.top * factor
            pieces = []
            for order, index in enumerate(active[place]):
                level, hi = groups[place][index]
                for j in range(2):
                    shift = choose(level, hi, j, top, -LOW)
                    weight = jnp.exp2(self.scores[place][2 * order + j] * factor - shift)
                    part = jnp.sum(weight, axis=0, keepdims=True)
                    self.total = part if self.total is None else self.total + part
                    pieces.append(low(weight))
            self.weights.append(jnp.concatenate(pieces, axis=0) if pieces else None)
            if place:
                for index in range(len(groups[place])):
                    value = jnp.zeros((2 * rows, span), jnp.bfloat16)
                    if index in active[place]:
                        at = active[place].index(index)
                        value = self.weights[place][2 * rows * at : 2 * rows * (at + 1)]
                    weight_refs[place - 1][self.number, 2 * rows * index : 2 * rows * (index + 1)] = value
            if pieces:
                part = mm(self.values([shards[place][index] for index in active[place]]), self.weights[place], TN)
                self.out_t = part if self.out_t is None else self.out_t + part

        def finish(self):
            inverse = 1.0 / self.total
            out_t = low(self.out_t * inverse)
            self.unstack(outs, out_t.T)
            delta = jnp.sum(wide(self.grads_t) * wide(out_t), axis=0, keepdims=True)
            spread = jnp.broadcast_to(inverse, (HD, span)).T
            queries_low = low(wide(self.queries) * (spread * scale))
            grads_low = low(wide(self.grads) * spread)
            gt_ref[self.number] = self.grads_t
            ql_ref[self.number] = queries_low
            gl_ref[self.number] = grads_low
            delta_ref[self.number] = delta
            factor_ref[self.number] = inverse * scale
            dq_ref[self.number] = self.back(
                [shards[0][index] for index in active[0]],
                self.weights[0],
                self.grads_t,
                delta,
                queries_low,
                grads_low,
                [homes[index] for index in active[0]],
            )

    def run(counted):
        active[:] = [[index for index, at in enumerate(part) if counted(at[0])] for part in groups]
        heads = [Forward(index, per, group, width) for index in range(per)]
        heads[0].start()
        heads[0].score()
        for index, head in enumerate(heads):
            after = heads[index + 1] if index + 1 < per else None
            if after:
                after.start()
                after.score()
            for place in places:
                head.weigh(place)
            head.finish()

    places = range(len(groups))
    active = []

    @pl.when(ctx >= 2)
    def _():
        run(lambda level: True)

    @pl.when(ctx < 2)
    def _():
        run(lambda level: level < 2)
        for index, (level, _) in enumerate(groups[0]):
            if level >= 2:
                homes[index][...] = jnp.zeros_like(homes[index])


def backward_kernel(groups, group, per, last, *refs):
    shards, refs = split(refs, groups)
    weight_refs, refs = refs[: len(groups)], refs[len(groups) :]
    gt_ref, ql_ref, gl_ref, delta_ref, factor_ref, dq_ref, *refs = refs
    dq_outs, refs = (refs[:2], refs[2:]) if last else (refs[:1], refs[1:])
    homes, refs = split(refs, groups)
    width = shards[0][0].shape[1] // 2
    for index in range(per):
        head = Head(index, per, group, width)
        at = head.number
        term = dq_ref[at]
        for place in range(len(groups)):
            term = term + head.back(
                shards[place],
                weight_refs[place][at],
                gt_ref[at],
                delta_ref[at],
                ql_ref[at],
                gl_ref[at],
                homes[place],
            )
        if last:
            head.unstack(dq_outs, low(term * factor_ref[at]).T)
        else:
            dq_outs[0][at] = term


def call(kernel, inputs, shapes, name, limit=12, grid=(), cost=None, in_spec=WHOLE, out_spec=WHOLE, scratch=()):
    return pl.pallas_call(
        kernel,
        grid=grid,
        out_shape=shapes,
        in_specs=in_spec if isinstance(in_spec, list) else [in_spec] * len(inputs),
        out_specs=[out_spec] * len(shapes),
        scratch_shapes=scratch,
        compiler_params=pltpu.CompilerParams(vmem_limit_bytes=limit * MIB),
        cost_estimate=cost,
        name=name,
    )(*inputs)


FREE = pl.CostEstimate(flops=0, bytes_accessed=0, transcendentals=0)


def merge(body, inputs, shapes, name):
    def kernel(*refs):
        body(refs[: len(inputs)], refs[len(inputs) :])

    return call(kernel, inputs, [like(shape) for shape in shapes], name)


def cost(keys, span, heads, matmuls):
    return pl.CostEstimate(flops=2 * keys * span * HD * heads * matmuls, bytes_accessed=0, transcendentals=0)


def sizes(others):
    return others[0].shape[0] // 2, len(others), others[0].shape[1] // HD


def forward(query, grad, others, held, groups):
    rows, heads, group = sizes(others)
    span = 2 * group * rows
    shards = [held[at] for part in groups for at in part]
    keys = shards[0].shape[0]
    per = heads
    steps = heads // per
    block = pl.BlockSpec((rows, per * group * HD), lambda step: (0, side() * steps + step))
    shapes = [like((rows, heads * group * HD))] * 2
    shapes += [like(shards[0].shape)] * len(groups[0])
    shapes += [like((heads, len(part) * keys, span)) for part in groups[1:]]
    shapes += [like((heads, HD, span)), like((heads, span, HD)), like((heads, span, HD))]
    shapes += [like((heads, 1, span), jnp.float32)] * 2 + [like((heads, HD, span), jnp.float32)]
    rest = call(
        lambda *refs: forward_kernel(groups, group, per, *refs),
        [query, grad, *others] + shards,
        shapes,
        "forward",
        limit=28,
        grid=(steps,),
        cost=cost(keys, span, heads, 2 * len(shards) + 4 * len(groups[0])),
        in_spec=[block] * 2 + [WHOLE] * (heads + len(shards)),
    )
    outs, rest = rest[:2], rest[2:]
    sums, rest = rest[: len(groups[0])], rest[len(groups[0]) :]
    return outs, sums, list(rest[: len(groups) - 1]), list(rest[len(groups) - 1 :])


def backward(others, held, groups, weights, state, last, after=()):
    rows, heads, group = sizes(others)
    span = 2 * group * rows
    shards = [held[at] for part in groups for at in part]
    keys = shards[0].shape[0]
    per = 2
    shapes = [like((rows, heads * group * HD))] * 2 if last else [like(state[-1].shape, state[-1].dtype)]
    heading = len(shapes)
    shapes += [like(shards[0].shape)] * len(shards)
    result = call(
        lambda *refs: backward_kernel(groups, group, per, last, *refs[len(after) :]),
        list(after) + shards + list(weights) + list(state),
        shapes,
        "backward",
        limit=14,
        grid=(heads // per,),
        cost=cost(keys, span, heads, 4 * len(shards)),
    )
    sums = dict(zip([at for part in groups for at in part], result[heading:]))
    return result[:heading], sums


def side():
    return lax.axis_index("kvh") % 2


def halves(array, place):
    rows, width = array.shape
    return pl.BlockSpec((rows, width // 2), lambda step: (0, side() ^ place))


def pack(query, grad, after, heads):
    rows, width = query.shape
    share = width // 2 // heads

    def kernel(query_ref, grad_ref, after_ref, *outs):
        for index, out in enumerate(outs):
            out[:rows] = query_ref[:, index * share : (index + 1) * share]
            out[rows:] = grad_ref[:, index * share : (index + 1) * share]

    specs = [halves(query, 1), halves(grad, 1), WHOLE]
    shapes = [like((2 * rows, share))] * heads
    return call(kernel, [query, grad, after], shapes, "pack", grid=(1,), in_spec=specs, cost=FREE)


def assemble(pairs):
    rows, half = pairs[0][0].shape
    inputs = [array for pair in pairs for array in pair]

    def kernel(*refs):
        outs, sems = refs[len(inputs) : -1], refs[-1]
        copies = []
        for index, ref in enumerate(refs[: len(inputs)]):
            start = pl.multiple_of((side() ^ (index % 2)) * half, half)
            target = outs[index // 2].at[:, pl.ds(start, half)]
            copies.append(pltpu.make_async_copy(ref, target, sems.at[index]))
        for copy in copies:
            copy.start()
        for copy in copies:
            copy.wait()

    return call(
        kernel,
        inputs,
        [like((rows, 2 * half))] * len(pairs),
        "assemble",
        out_spec=HBM,
        scratch=[pltpu.SemaphoreType.DMA((len(inputs),))],
    )


def permute(array, target, wrap=True):
    blocks, peers = lax.axis_size("ctx"), lax.axis_size("kvh")
    pairs = []
    for c in range(blocks):
        for k in range(peers):
            to_c, to_k = target(c, k)
            if wrap or 0 <= to_c < blocks:
                pairs.append((c * peers + k, to_c % blocks * peers + to_k))
    return lax.ppermute(array, AXES, pairs)


def along(array, by, wrap=True):
    return permute(array, lambda c, k: (c + by, k), wrap)


def pair_swap(array):
    return permute(array, lambda c, k: (c ^ 1, k))


def across(array):
    return permute(array, lambda c, k: (c, k ^ 2))


def sibling(array):
    return permute(array, lambda c, k: (c, k ^ 1))


def gather(own, levels):
    odd = is_odd()
    held = {(0, 0): own}
    held[2, 0] = along(own, 2)
    held[0, 2] = across(own)
    for level in range(3, levels):
        held[level, 0] = along(held[level - 1, 0], 1 << (level - 2))
    held[2, 2] = across(held[2, 0])
    held[1, 0] = pair_swap(jnp.where(odd, held[2, 0], own))
    for level in range(3, levels):
        held[level, 2] = across(held[level, 0])
    held[1, 2] = pair_swap(jnp.where(odd, held[2, 2], held[0, 2]))
    return held


def shards(query_act, key_act, value_act, grad_out):
    blocks, peers = lax.axis_size("ctx"), lax.axis_size("kvh")
    assert peers == 4, peers
    levels = (blocks - 1).bit_length() + 1
    later = range(3, levels)
    rows, width = key_act.shape
    shape = (2 * rows, width)

    def part(place):
        half = width // 2
        start = (side() ^ place) * half
        return jnp.concatenate(
            [lax.dynamic_slice_in_dim(array, start, half, 1) for array in (key_act, value_act)], axis=1
        )

    kept, sent = part(0), part(1)

    def stack(ins, outs):
        outs[0][:rows] = ins[0][...]
        outs[0][rows:] = ins[1][...]

    (own,) = merge(stack, [kept, sibling(sent)], [shape], "stack")
    held = gather(own, levels)
    heads = width // (2 * HD)
    others = [sibling(array) for array in pack(query_act, grad_out, held[0, 2], heads)]

    group_a = [(level, 2) for level in later] + [(1, 2)]
    group_b = [(2, 2), (0, 2)] + [(level, 0) for level in later] + [(1, 0)]
    group_d = [(2, 0), (0, 0)]
    outs, sums_a, weights, state = forward(query_act, grad_out, others, held, [group_a, group_b, group_d])
    *far_2, near_2 = sums_a
    got_far = [across(array) for array in far_2]
    got_near = pair_swap(near_2)
    (dq_t,), sums = backward(others, held, [group_b], weights[:1], state, False)
    got_out = sibling(outs[1])

    def second(ins, outs):
        for index, out in enumerate(outs):
            out[...] = low(wide(ins[2 * index][...]) + wide(ins[2 * index + 1][...]))

    far_0 = [array for pair in zip([sums[level, 0] for level in later], got_far) for array in pair]
    far_0 = merge(second, far_0, [shape] * len(later), "second")

    def aside(ins, outs):
        two, zero, swapped = ins
        from_pair = wide(swapped[...])
        odd = is_odd()
        none = jnp.zeros_like(from_pair)
        outs[0][...] = low(wide(two[...]) + jnp.where(odd, from_pair, none))
        outs[1][...] = low(wide(zero[...]) + jnp.where(odd, none, from_pair))

    two_2, zero_2 = merge(
        aside, [sums[2, 2], sums[0, 2], got_near], [shape] * 2, "aside"
    )
    chain = far_0[-1]
    for level in range(levels - 1, 3, -1):
        chain = low(wide(far_0[level - 4]) + wide(along(chain, -(1 << (level - 2)))))
    got_chain = along(chain, -2, False)
    got_two = across(two_2)
    got_one = pair_swap(sums[1, 0])
    dqs, last_sums = backward(others, held, [group_d], weights[1:], state[:-1] + [dq_t], True, [two_2])
    got_dq = sibling(dqs[1])

    def third(ins, outs):
        base, chain, two, one = ins
        from_pair = wide(one[...])
        terms = jnp.where(is_odd(), from_pair, jnp.zeros_like(from_pair))
        outs[0][...] = low(wide(base[...]) + wide(chain[...]) + wide(two[...]) + terms)

    (two_0,) = merge(third, [last_sums[2, 0], got_chain, got_two, got_one], [shape], "third")
    got_chain = along(two_0, -2, False)
    got_zero = across(zero_2)
    out, grad_query = assemble([(outs[0], got_out), (dqs[0], got_dq)])

    def fourth(ins, outs):
        base, one, zero, chain = ins[:4]
        from_pair = wide(one[...])
        terms = jnp.where(is_odd(), jnp.zeros_like(from_pair), from_pair)
        total = low(wide(base[...]) + wide(chain[...]) + wide(zero[...]) + terms)
        outs[0][...] = total[:rows]
        outs[1][...] = total[rows:]

    kept, sent = merge(
        fourth,
        [last_sums[0, 0], got_one, got_zero, got_chain],
        [(rows, width)] * 2,
        "fourth",
    )

    def fifth(ins, outs):
        half = width // 2
        for place, ref in enumerate(ins):
            at = pl.ds(pl.multiple_of((side() ^ place) * half, half), half)
            outs[0][:, at] = ref[:, :half]
            outs[1][:, at] = ref[:, half:]

    grad_key, grad_value = merge(fifth, [kept, sibling(sent)], [(rows, width)] * 2, "fifth")
    return out, grad_query, grad_key, grad_value


def solution(mesh):
    spec = P(AXES, None)
    return jax.shard_map(
        shards, mesh=mesh, in_specs=(spec,) * 4, out_specs=(spec,) * 4, check_vma=False
    )
```

```python
import jax
import jax.numpy as jnp
from jax import lax
from jax.experimental import pallas as pl
from jax.experimental.pallas import tpu as pltpu
from jax.sharding import PartitionSpec as P

HD = 128
LOG2E = 1.4426950408889634
LOW = -1e30

NN = (((1,), (0,)), ((), ()))
TN = (((0,), (0,)), ((), ()))

MIB = 2**20
AXES = ("ctx", "kvh")
WHOLE = pl.BlockSpec(memory_space=pltpu.VMEM)
HBM = pl.BlockSpec(memory_space=pltpu.HBM)


def mm(a, b, dims):
    return lax.dot_general(a, b, dims, preferred_element_type=jnp.float32)


def wide(value):
    return value.astype(jnp.float32)


def low(value):
    return value.astype(jnp.bfloat16)


def like(shape, dtype=jnp.bfloat16):
    return jax.ShapeDtypeStruct(shape, dtype)


def is_odd():
    return lax.axis_index("ctx") % 2 == 1


class Head:
    def __init__(self, index, per, group, width):
        self.index = index
        self.number = pl.program_id(0) * per + index
        self.group = group
        self.first = self.number * group * HD
        self.at_k = pl.ds(pl.multiple_of(self.number * HD, HD), HD)
        self.at_v = pl.ds(pl.multiple_of(self.number * HD + width, HD), HD)

    def column(self, r):
        return pl.ds(pl.multiple_of(self.first + r * HD, HD), HD)

    def keys(self, shards):
        return jnp.concatenate([ref[:, self.at_k] for ref in shards], axis=0)

    def values(self, shards):
        return jnp.concatenate([ref[:, self.at_v] for ref in shards], axis=0)

    def stack(self, mine, other, at):
        base = self.index * self.group
        blocks = [mine[:, (base + r) * HD : (base + r + 1) * HD] for r in range(self.group)]
        each = other[0].shape[1] // (self.group * HD)
        piece, base = other[self.index // each], self.index % each * self.group
        blocks += [piece[at, (base + r) * HD : (base + r + 1) * HD] for r in range(self.group)]
        return jnp.concatenate(blocks, axis=0)

    def unstack(self, refs, value):
        rows = refs[0].shape[0]
        for side, ref in enumerate(refs):
            for r in range(self.group):
                at = (side * self.group + r) * rows
                ref[:, self.column(r)] = value[at : at + rows]

    def back(self, shards, weights, grads_t, delta, queries_low, grads_low, homes):
        rows = shards[0].shape[0]
        grad_prob = mm(self.values(shards), grads_t, NN) - delta
        grad_scores = weights * low(grad_prob)
        term = mm(self.keys(shards), grad_scores, TN)
        grad_k = low(mm(grad_scores, queries_low, NN))
        grad_v = low(mm(weights, grads_low, NN))
        for index, ref in enumerate(homes):
            part = slice(index * rows, (index + 1) * rows)
            ref[:, self.at_k] = grad_k[part]
            ref[:, self.at_v] = grad_v[part]
        return term


def split(refs, groups):
    parts = []
    for part in groups:
        parts.append(refs[: len(part)])
        refs = refs[len(part) :]
    return parts, refs


def forward_kernel(groups, group, per, pieces, *refs):
    q_ref, g_ref = refs[:2]
    others, refs = refs[2 : 2 + pieces], refs[2 + pieces :]
    shards, refs = split(refs, groups)
    outs, refs = refs[:2], refs[2:]
    homes, refs = refs[: len(groups[0])], refs[len(groups[0]) :]
    weight_refs, refs = refs[: len(groups) - 1], refs[len(groups) - 1 :]
    gt_ref, ql_ref, gl_ref, delta_ref, factor_ref, dq_ref = refs
    rows = q_ref.shape[0]
    width = shards[0][0].shape[1] // 2
    half = group * rows
    span = 2 * half
    scale = HD ** (-0.5)
    factor = scale * LOG2E
    ctx = lax.axis_index("ctx")
    kvh = lax.axis_index("kvh")
    key_pos = lax.broadcasted_iota(jnp.int32, (rows, span), 0)
    column = lax.broadcasted_iota(jnp.int32, (rows, span), 1)
    causal = key_pos <= column % rows
    own = lax.broadcasted_iota(jnp.int32, (1, span), 1) < half
    diagonal = [causal | (column >= half), causal | (column < half)]

    def choose(level, hi, j, value, other):
        if level:
            return jnp.where(ctx >= (1 << (level - 1)), value, other)
        sides = []
        for i in range(2):
            if hi == 0 and i == j:
                sides.append(value)
            else:
                before = lax.bitwise_xor(kvh, hi ^ j) < lax.bitwise_xor(kvh, i)
                sides.append(jnp.where(before, value, other))
        return jnp.where(own, sides[0], sides[1])

    class Forward(Head):
        def start(self):
            self.queries = self.stack(q_ref, others, slice(0, rows))
            self.grads = self.stack(g_ref, others, slice(rows, 2 * rows))
            self.queries_t, self.grads_t = self.queries.T, self.grads.T
            self.top, self.total, self.out_t = None, None, None
            self.scores, self.weights = [], []

        def score(self):
            used = [shards[place][index] for place in places for index in active[place]]
            raw = mm(self.keys(used), self.queries_t, NN)
            at = 0
            for place in places:
                pieces = []
                for index in active[place]:
                    level, hi = groups[place][index]
                    for j in range(2):
                        piece = raw[at : at + rows]
                        at += rows
                        if level == 0 and hi == 0:
                            piece = jnp.where(diagonal[j], piece, LOW)
                        best = choose(level, hi, j, jnp.max(piece, axis=0, keepdims=True), LOW)
                        self.top = best if self.top is None else jnp.maximum(self.top, best)
                        pieces.append(piece)
                self.scores.append(pieces)

        def weigh(self, place):
            top = self.top * factor
            pieces = []
            for order, index in enumerate(active[place]):
                level, hi = groups[place][index]
                for j in range(2):
                    shift = choose(level, hi, j, top, -LOW)
                    weight = jnp.exp2(self.scores[place][2 * order + j] * factor - shift)
                    part = jnp.sum(weight, axis=0, keepdims=True)
                    self.total = part if self.total is None else self.total + part
                    pieces.append(low(weight))
            self.weights.append(jnp.concatenate(pieces, axis=0) if pieces else None)
            if place:
                for index in range(len(groups[place])):
                    value = jnp.zeros((2 * rows, span), jnp.bfloat16)
                    if index in active[place]:
                        at = active[place].index(index)
                        value = self.weights[place][2 * rows * at : 2 * rows * (at + 1)]
                    weight_refs[place - 1][self.number, 2 * rows * index : 2 * rows * (index + 1)] = value
            if pieces:
                part = mm(self.values([shards[place][index] for index in active[place]]), self.weights[place], TN)
                self.out_t = part if self.out_t is None else self.out_t + part

        def finish(self):
            inverse = 1.0 / self.total
            out_t = low(self.out_t * inverse)
            self.unstack(outs, out_t.T)
            delta = jnp.sum(wide(self.grads_t) * wide(out_t), axis=0, keepdims=True)
            spread = jnp.broadcast_to(inverse, (HD, span)).T
            queries_low = low(wide(self.queries) * (spread * scale))
            grads_low = low(wide(self.grads) * spread)
            gt_ref[self.number] = self.grads_t
            ql_ref[self.number] = queries_low
            gl_ref[self.number] = grads_low
            delta_ref[self.number] = delta
            factor_ref[self.number] = inverse * scale
            dq_ref[self.number] = self.back(
                [shards[0][index] for index in active[0]],
                self.weights[0],
                self.grads_t,
                delta,
                queries_low,
                grads_low,
                [homes[index] for index in active[0]],
            )

    def run(counted):
        active[:] = [[index for index, at in enumerate(part) if counted(at[0])] for part in groups]
        heads = [Forward(index, per, group, width) for index in range(per)]
        heads[0].start()
        heads[0].score()
        for index, head in enumerate(heads):
            after = heads[index + 1] if index + 1 < per else None
            if after:
                after.start()
                after.score()
            for place in places:
                head.weigh(place)
            head.finish()

    places = range(len(groups))
    active = []

    @pl.when(ctx >= 2)
    def _():
        run(lambda level: True)

    @pl.when(ctx < 2)
    def _():
        run(lambda level: level < 2)
        for index, (level, _) in enumerate(groups[0]):
            if level >= 2:
                homes[index][...] = jnp.zeros_like(homes[index])


def backward_kernel(groups, group, per, last, *refs):
    shards, refs = split(refs, groups)
    weight_refs, refs = refs[: len(groups)], refs[len(groups) :]
    gt_ref, ql_ref, gl_ref, delta_ref, factor_ref, dq_ref, *refs = refs
    dq_outs, refs = (refs[:2], refs[2:]) if last else (refs[:1], refs[1:])
    homes, refs = split(refs, groups)
    width = shards[0][0].shape[1] // 2
    for index in range(per):
        head = Head(index, per, group, width)
        at = head.number
        term = dq_ref[at]
        for place in range(len(groups)):
            term = term + head.back(
                shards[place],
                weight_refs[place][at],
                gt_ref[at],
                delta_ref[at],
                ql_ref[at],
                gl_ref[at],
                homes[place],
            )
        if last:
            head.unstack(dq_outs, low(term * factor_ref[at]).T)
        else:
            dq_outs[0][at] = term


def call(kernel, inputs, shapes, name, limit=12, grid=(), cost=None, in_spec=WHOLE, out_spec=WHOLE, scratch=()):
    return pl.pallas_call(
        kernel,
        grid=grid,
        out_shape=shapes,
        in_specs=in_spec if isinstance(in_spec, list) else [in_spec] * len(inputs),
        out_specs=[out_spec] * len(shapes),
        scratch_shapes=scratch,
        compiler_params=pltpu.CompilerParams(vmem_limit_bytes=limit * MIB),
        cost_estimate=cost,
        name=name,
    )(*inputs)


FREE = pl.CostEstimate(flops=0, bytes_accessed=0, transcendentals=0)


def merge(body, inputs, shapes, name):
    def kernel(*refs):
        body(refs[: len(inputs)], refs[len(inputs) :])

    return call(kernel, inputs, [like(shape) for shape in shapes], name)


def cost(keys, span, heads, matmuls):
    return pl.CostEstimate(flops=2 * keys * span * HD * heads * matmuls, bytes_accessed=0, transcendentals=0)


def sizes(others, shard):
    heads = shard.shape[1] // (2 * HD)
    return others[0].shape[0] // 2, heads, len(others) * others[0].shape[1] // (heads * HD)


def forward(query, grad, others, held, groups):
    rows, heads, group = sizes(others, held[0, 0])
    span = 2 * group * rows
    shards = [held[at] for part in groups for at in part]
    keys = shards[0].shape[0]
    per = heads
    steps = heads // per
    block = pl.BlockSpec((rows, per * group * HD), lambda step: (0, side() * steps + step))
    shapes = [like((rows, heads * group * HD))] * 2
    shapes += [like(shards[0].shape)] * len(groups[0])
    shapes += [like((heads, len(part) * keys, span)) for part in groups[1:]]
    shapes += [like((heads, HD, span)), like((heads, span, HD)), like((heads, span, HD))]
    shapes += [like((heads, 1, span), jnp.float32)] * 2 + [like((heads, HD, span), jnp.float32)]
    rest = call(
        lambda *refs: forward_kernel(groups, group, per, len(others), *refs),
        [query, grad, *others] + shards,
        shapes,
        "forward",
        limit=28,
        grid=(steps,),
        cost=cost(keys, span, heads, 2 * len(shards) + 4 * len(groups[0])),
        in_spec=[block] * 2 + [WHOLE] * (len(others) + len(shards)),
    )
    outs, rest = rest[:2], rest[2:]
    sums, rest = rest[: len(groups[0])], rest[len(groups[0]) :]
    return outs, sums, list(rest[: len(groups) - 1]), list(rest[len(groups) - 1 :])


def backward(others, held, groups, weights, state, last, after=()):
    rows, heads, group = sizes(others, held[0, 0])
    span = 2 * group * rows
    shards = [held[at] for part in groups for at in part]
    keys = shards[0].shape[0]
    per = 2
    shapes = [like((rows, heads * group * HD))] * 2 if last else [like(state[-1].shape, state[-1].dtype)]
    heading = len(shapes)
    shapes += [like(shards[0].shape)] * len(shards)
    result = call(
        lambda *refs: backward_kernel(groups, group, per, last, *refs[len(after) :]),
        list(after) + shards + list(weights) + list(state),
        shapes,
        "backward",
        limit=14,
        grid=(heads // per,),
        cost=cost(keys, span, heads, 4 * len(shards)),
    )
    sums = dict(zip([at for part in groups for at in part], result[heading:]))
    return result[:heading], sums


def side():
    return lax.axis_index("kvh") % 2


def halves(array, place):
    rows, width = array.shape
    return pl.BlockSpec((rows, width // 2), lambda step: (0, side() ^ place))


def pack(query, grad, after, pieces):
    rows, width = query.shape
    share = width // 2 // pieces

    def kernel(query_ref, grad_ref, after_ref, *outs):
        for index, out in enumerate(outs):
            out[:rows] = query_ref[:, index * share : (index + 1) * share]
            out[rows:] = grad_ref[:, index * share : (index + 1) * share]

    specs = [halves(query, 1), halves(grad, 1), WHOLE]
    shapes = [like((2 * rows, share))] * pieces
    return call(kernel, [query, grad, after], shapes, "pack", grid=(1,), in_spec=specs, cost=FREE)


def assemble(pairs):
    rows, half = pairs[0][0].shape
    inputs = [array for pair in pairs for array in pair]

    def kernel(*refs):
        outs, sems = refs[len(inputs) : -1], refs[-1]
        copies = []
        for index, ref in enumerate(refs[: len(inputs)]):
            start = pl.multiple_of((side() ^ (index % 2)) * half, half)
            target = outs[index // 2].at[:, pl.ds(start, half)]
            copies.append(pltpu.make_async_copy(ref, target, sems.at[index]))
        for copy in copies:
            copy.start()
        for copy in copies:
            copy.wait()

    return call(
        kernel,
        inputs,
        [like((rows, 2 * half))] * len(pairs),
        "assemble",
        out_spec=HBM,
        scratch=[pltpu.SemaphoreType.DMA((len(inputs),))],
    )


def permute(array, target, wrap=True):
    blocks, peers = lax.axis_size("ctx"), lax.axis_size("kvh")
    pairs = []
    for c in range(blocks):
        for k in range(peers):
            to_c, to_k = target(c, k)
            if wrap or 0 <= to_c < blocks:
                pairs.append((c * peers + k, to_c % blocks * peers + to_k))
    return lax.ppermute(array, AXES, pairs)


def along(array, by, wrap=True):
    return permute(array, lambda c, k: (c + by, k), wrap)


def pair_swap(array):
    return permute(array, lambda c, k: (c ^ 1, k))


def across(array):
    return permute(array, lambda c, k: (c, k ^ 2))


def sibling(array):
    return permute(array, lambda c, k: (c, k ^ 1))


def gather(own, levels):
    odd = is_odd()
    held = {(0, 0): own}
    held[2, 0] = along(own, 2)
    held[0, 2] = across(own)
    for level in range(3, levels):
        held[level, 0] = along(held[level - 1, 0], 1 << (level - 2))
    held[2, 2] = across(held[2, 0])
    held[1, 0] = pair_swap(jnp.where(odd, held[2, 0], own))
    for level in range(3, levels):
        held[level, 2] = across(held[level, 0])
    held[1, 2] = pair_swap(jnp.where(odd, held[2, 2], held[0, 2]))
    return held


def shards(query_act, key_act, value_act, grad_out):
    blocks, peers = lax.axis_size("ctx"), lax.axis_size("kvh")
    assert peers == 4, peers
    levels = (blocks - 1).bit_length() + 1
    later = range(3, levels)
    rows, width = key_act.shape
    shape = (2 * rows, width)

    def part(place):
        half = width // 2
        start = (side() ^ place) * half
        return jnp.concatenate(
            [lax.dynamic_slice_in_dim(array, start, half, 1) for array in (key_act, value_act)], axis=1
        )

    kept, sent = part(0), part(1)

    def stack(ins, outs):
        outs[0][:rows] = ins[0][...]
        outs[0][rows:] = ins[1][...]

    (own,) = merge(stack, [kept, sibling(sent)], [shape], "stack")
    held = gather(own, levels)
    heads = width // (2 * HD)
    others = [sibling(array) for array in pack(query_act, grad_out, held[0, 2], heads // 2)]

    group_a = [(level, 2) for level in later] + [(1, 2)]
    group_b = [(2, 2), (0, 2)] + [(level, 0) for level in later] + [(1, 0)]
    group_d = [(2, 0), (0, 0)]
    outs, sums_a, weights, state = forward(query_act, grad_out, others, held, [group_a, group_b, group_d])
    *far_2, near_2 = sums_a
    got_far = [across(array) for array in far_2]
    got_near = pair_swap(near_2)
    (dq_t,), sums = backward(others, held, [group_b], weights[:1], state, False)
    got_out = sibling(outs[1])

    def second(ins, outs):
        for index, out in enumerate(outs):
            out[...] = low(wide(ins[2 * index][...]) + wide(ins[2 * index + 1][...]))

    far_0 = [array for pair in zip([sums[level, 0] for level in later], got_far) for array in pair]
    far_0 = merge(second, far_0, [shape] * len(later), "second")

    def aside(ins, outs):
        two, zero, swapped = ins
        from_pair = wide(swapped[...])
        odd = is_odd()
        none = jnp.zeros_like(from_pair)
        outs[0][...] = low(wide(two[...]) + jnp.where(odd, from_pair, none))
        outs[1][...] = low(wide(zero[...]) + jnp.where(odd, none, from_pair))

    two_2, zero_2 = merge(
        aside, [sums[2, 2], sums[0, 2], got_near], [shape] * 2, "aside"
    )
    chain = far_0[-1]
    for level in range(levels - 1, 3, -1):
        chain = low(wide(far_0[level - 4]) + wide(along(chain, -(1 << (level - 2)))))
    got_chain = along(chain, -2, False)
    got_two = across(two_2)
    got_one = pair_swap(sums[1, 0])
    dqs, last_sums = backward(others, held, [group_d], weights[1:], state[:-1] + [dq_t], True, [two_2])
    got_dq = sibling(dqs[1])

    def third(ins, outs):
        base, chain, two, one = ins
        from_pair = wide(one[...])
        terms = jnp.where(is_odd(), from_pair, jnp.zeros_like(from_pair))
        outs[0][...] = low(wide(base[...]) + wide(chain[...]) + wide(two[...]) + terms)

    (two_0,) = merge(third, [last_sums[2, 0], got_chain, got_two, got_one], [shape], "third")
    got_chain = along(two_0, -2, False)
    got_zero = across(zero_2)
    out, grad_query = assemble([(outs[0], got_out), (dqs[0], got_dq)])

    def fourth(ins, outs):
        base, one, zero, chain = ins[:4]
        from_pair = wide(one[...])
        terms = jnp.where(is_odd(), jnp.zeros_like(from_pair), from_pair)
        total = low(wide(base[...]) + wide(chain[...]) + wide(zero[...]) + terms)
        outs[0][...] = total[:rows]
        outs[1][...] = total[rows:]

    kept, sent = merge(
        fourth,
        [last_sums[0, 0], got_one, got_zero, got_chain],
        [(rows, width)] * 2,
        "fourth",
    )

    def fifth(ins, outs):
        half = width // 2
        for place, ref in enumerate(ins):
            at = pl.ds(pl.multiple_of((side() ^ place) * half, half), half)
            outs[0][:, at] = ref[:, :half]
            outs[1][:, at] = ref[:, half:]

    grad_key, grad_value = merge(fifth, [kept, sibling(sent)], [(rows, width)] * 2, "fifth")
    return out, grad_query, grad_key, grad_value


def solution(mesh):
    spec = P(AXES, None)
    return jax.shard_map(
        shards, mesh=mesh, in_specs=(spec,) * 4, out_specs=(spec,) * 4, check_vma=False
    )
```
